256 devices in a mesh: pair: 8 (over x, core), tile: 32 (over z, y).
Axes of the slice: x: 4, y: 4, z: 8, core: 2. Of those that a mesh axis runs over, the one named last changes fastest.
Arguments:
- amplitudes: bfloat16 [4096, 32, 256], P('pair', 'tile'), may hold values from -6 to 6
- size_cd: int32 [32], P('tile'), may hold values from 64 to 256, as said below
- integrals: bfloat16 [1024, 256, 256], P('tile'), may hold values from -0.125 to 0.125
- block_rows: int32 [1024], P('tile'), may hold values from 0 to 63, as said below
- block_cols: int32 [1024], P('tile'), may hold values from 0 to 31
- size_ab: int32 [64], P('tile'), may hold values from 64 to 256, as said below
- mirror: int32 [4096], replicated, may hold values from 0 to 4095, as said below
Outputs:
- symmetrized: bfloat16 [4096, 64, 256], P('pair', 'tile')
The draws below stay inside these ranges and needn't reach their ends.
Inputs may be any that keep to these rules, and one draw needn't show every extreme that they name: `block_rows`: each block's row tile and column tile carry the same irreducible representation. Of the 32 blocks of one device of tile (aligned runs), at most 2 name row tiles d * 2 to (d + 1) * 2 - 1 of any one owner d, and exactly 2 for some owner. mirror[mirror[k]] = k and mirror[k] != k. `size_cd`: tile 0 is full. `size_ab`: tile 0 is full.
All inputs are finite; a program needn't handle non-finite values.
Results may differ from the reference program's by a relative error of at most 0.0059.
Values may be sent and summed in bfloat16 or wider, within the bound.
No kernel may reach another device: no remote copies, remote signals or barrier semaphores. Data moves between devices by JAX's collectives and lax.ppermute only.
A program may use at most 128 MiB of HBM per device.

```python
import jax
import jax.numpy as jnp
from jax import lax

TS = 256
AT_DEV = 2
BLK_DEV = 32
NPAIR = 4096
NC = 32
NA = 64
NBLK = 1024
N_TILE = 32


def route_tables(key):
    dest_key, count_key, hot_key, within_key, irrep_key, shuffle_key, member_key = jax.random.split(key, 7)
    capacity = max(2, 2 * BLK_DEV // N_TILE)
    lowest = max(1, -(-(BLK_DEV - N_TILE) // (capacity - 1)))
    highest = BLK_DEV // capacity
    owners = jnp.arange(N_TILE, dtype=jnp.int32)
    scores = jax.random.randint(dest_key, (N_TILE, N_TILE), 0, 1 << 20) * N_TILE + owners[None, :]
    hottest = jax.random.randint(hot_key, (), 0, N_TILE)
    scores = scores + (owners[None, :] == hottest).astype(jnp.int32) * (1 << 26)
    order = jnp.argsort(-scores, axis=1)
    doubled = jax.random.randint(count_key, (N_TILE, 1), lowest, highest + 1)
    column = jnp.arange(BLK_DEV, dtype=jnp.int32)[None, :]
    rank_owner = jnp.where(column < capacity * doubled, column // capacity, column - (capacity - 1) * doubled)
    owner = jnp.take_along_axis(order, rank_owner, axis=1)
    within = jax.random.randint(within_key, (N_TILE, BLK_DEV), 0, AT_DEV)
    rows = (owner * AT_DEV + within).reshape(-1).astype(jnp.int32)
    irrep_rows = jax.random.randint(irrep_key, (NA,), 0, 8)
    shuffled = jax.random.permutation(shuffle_key, NC)
    inverse = jnp.argsort(shuffled)
    member = jax.random.randint(member_key, (NBLK,), 0, NC // 8)
    cols = inverse[irrep_rows[rows] + 8 * member].astype(jnp.int32)
    return (rows, cols)


def draw_block_rows(key, part):
    rows, cols = route_tables(key)
    return rows


def draw_block_cols(key, part):
    rows, cols = route_tables(key)
    return cols


def draw_mirror(key, part):
    key = jax.random.fold_in(key, 11)
    shuffled = jax.random.permutation(key, NPAIR).astype(jnp.int32)
    flipped = jnp.arange(NPAIR, dtype=jnp.int32) ^ 1
    return jnp.zeros((NPAIR,), jnp.int32).at[shuffled].set(shuffled[flipped])


def draw_size_cd(key, part):
    key = jax.random.fold_in(key, 12)
    sizes = jax.random.randint(key, (NC,), TS // 4, TS + 1).astype(jnp.int32)
    return sizes.at[0].set(TS)


def draw_size_ab(key, part):
    key = jax.random.fold_in(key, 13)
    sizes = jax.random.randint(key, (NA,), TS // 4, TS + 1).astype(jnp.int32)
    return sizes.at[0].set(TS)


def shard_levels(own_key, extent, pieces, low, high):
    def one(dim, parts):
        heights = jax.random.uniform(jax.random.fold_in(jax.random.fold_in(own_key, 6), dim), (parts,), jnp.float32, low / len(pieces), high / len(pieces))
        return jnp.repeat(jnp.exp(heights), extent[dim] // parts).reshape((-1,) + (1,) * (len(extent) - dim - 1))

    level = one(*pieces[0])
    for cut in pieces[1:]:
        level = level * one(*cut)
    return level


def gaussian(key, shape, spread, bound, shards=(), kind=jnp.bfloat16):
    values = jax.random.normal(key, shape, jnp.float32) * spread
    if len(shards) > 0:
        values = shard_levels(key, shape, shards, -0.22, 0.18) * values
    return jnp.clip(values, min=-bound, max=bound).astype(kind)


def setup_inputs(seed: int = 0) -> dict:
    key_of = jax.random.split(jax.random.key(seed), 8)
    amplitudes = gaussian(key_of[0], (NPAIR, NC, TS), 1.0, 6.0, ((0, 8), (1, 32)))
    size_cd = draw_size_cd(jax.random.fold_in(key_of[7], 71), 0)
    integrals = gaussian(key_of[2], (NBLK, TS, TS), (TS * 8) ** -0.5, 0.125, ((0, 32),))
    block_rows = draw_block_rows(jax.random.fold_in(key_of[7], 71), 0)
    block_cols = draw_block_cols(jax.random.fold_in(key_of[7], 71), 0)
    size_ab = draw_size_ab(jax.random.fold_in(key_of[7], 71), 0)
    mirror = draw_mirror(jax.random.fold_in(key_of[7], 71), 0)
    return dict(amplitudes=amplitudes, size_cd=size_cd, integrals=integrals, block_rows=block_rows, block_cols=block_cols, size_ab=size_ab, mirror=mirror)


def reference(amplitudes, size_cd, integrals, block_rows, block_cols, size_ab, mirror):
    position = lax.broadcasted_iota(jnp.int32, (1, NC, TS), 2)
    masked = jnp.where(position < size_cd[None, :, None], amplitudes, jnp.zeros_like(amplitudes))

    def add_block(total, item):
        weight, row_tile, col_tile = item
        chosen = lax.dynamic_index_in_dim(masked, col_tile, 1, keepdims=False)
        term = jnp.dot(chosen, weight.T, preferred_element_type=jnp.float32).astype(jnp.bfloat16)
        term_wide = lax.optimization_barrier(term).astype(jnp.float32)
        current = lax.dynamic_index_in_dim(total, row_tile, 1, keepdims=False)
        total = lax.dynamic_update_index_in_dim(total, current + term_wide, row_tile, 1)
        return total, None

    start_total = jnp.zeros((NPAIR, NA, TS), jnp.float32)
    total, unused = lax.scan(add_block, start_total, (integrals, block_rows, block_cols))
    live_mask = lax.broadcasted_iota(jnp.int32, (1, NA, TS), 2) < size_ab[None, :, None]
    ladder = jnp.where(live_mask, total, jnp.zeros_like(total)).astype(jnp.bfloat16)
    ladder_wide = lax.optimization_barrier(ladder).astype(jnp.float32)
    return (ladder_wide + ladder_wide[mirror]).astype(jnp.bfloat16)
```

```python
import functools

import jax
import jax.numpy as jnp
from jax import lax
from jax.experimental import pallas as pl
from jax.experimental.pallas import tpu as pltpu
from jax.sharding import PartitionSpec as P

NZ, NY = 8, 4
LABEL_ROWS = 8


def ring_pairs(axis, shift):
    pairs = []
    for z in range(NZ):
        for y in range(NY):
            to = ((z + shift) % NZ, y) if axis == "z" else (z, (y + shift) % NY)
            pairs.append((z * NY + y, to[0] * NY + to[1]))
    return pairs


def ring_gather(axis, piece):
    size = NZ if axis == "z" else NY
    ahead, back = ring_pairs(axis, 1), ring_pairs(axis, -1)
    parts = {0: [piece]}
    left = right = piece
    for step in range(1, size // 2):
        left = lax.ppermute(left, "tile", ahead)
        right = lax.ppermute(right, "tile", back)
        parts[step], parts[size - step] = [left], [right]
    half = piece.shape[0] // 2
    parts[size // 2] = [
        lax.ppermute(left[:half], "tile", ahead),
        lax.ppermute(right[half:], "tile", back),
    ]
    return [p for s in range(size) for p in parts[s]]


def route_kernel(rows_ref, cols_ref, share_ref, w_ref, o_ref, count):
    owners, height, width = o_ref.shape
    blocks, share, _ = w_ref.shape
    o_ref[...] = jnp.zeros_like(o_ref)
    for d in range(owners):
        count[d] = 0
    line = lax.broadcasted_iota(jnp.int32, (LABEL_ROWS, width), 0)
    for b in range(blocks):
        row = rows_ref[b]
        owner = row // 2
        rank = count[owner]
        count[owner] = rank + 1
        o_ref[owner, pl.ds(pl.multiple_of(rank * share, share), share), :] = w_ref[b]
        tags = o_ref[owner, 2 * share :, :].astype(jnp.float32)
        tags = jnp.where(line == 2 * rank, (row % 2 + 1).astype(jnp.float32), tags)
        tags = jnp.where(line == 2 * rank + 1, cols_ref[b].astype(jnp.float32), tags)
        o_ref[owner, 2 * share :, :] = tags.astype(jnp.bfloat16)


def route(block_rows, block_cols, share_id, integrals, owners, shares):
    blocks, height, width = integrals.shape
    share = height // shares
    return pl.pallas_call(
        route_kernel,
        grid_spec=pltpu.PrefetchScalarGridSpec(
            num_scalar_prefetch=3,
            grid=(1,),
            in_specs=[pl.BlockSpec((blocks, share, width), lambda i, r, c, s: (0, s[0], 0))],
            out_specs=pl.BlockSpec((owners, 2 * share + LABEL_ROWS, width), lambda i, r, c, s: (0, 0, 0)),
            scratch_shapes=[pltpu.SMEM((owners,), jnp.int32)],
        ),
        out_shape=jax.ShapeDtypeStruct((owners, 2 * share + LABEL_ROWS, width), jnp.bfloat16),
        compiler_params=pltpu.CompilerParams(vmem_limit_bytes=16 << 20),
    )(block_rows, block_cols, share_id, integrals)


def mirror_kernel(first_ref, live_ref, mirror_ref, all_ref, a_ref, b_ref, *, step):
    total_pairs, width = all_ref.shape
    count = a_ref.shape[0]
    live = lax.broadcasted_iota(jnp.int32, (1, width), 1) < live_ref[0]
    for part, out in enumerate((a_ref, b_ref)):
        me = lax.broadcasted_iota(jnp.int32, (count, step), 0) + (first_ref[0] + part * count)
        total = jnp.zeros((count, width), jnp.float32)
        for at in range(0, total_pairs, step):
            here = lax.broadcasted_iota(jnp.int32, (count, step), 1) + at
            pick = (mirror_ref[:, at : at + step] == me) | (here == me)
            pick = jnp.where(pick, 1.0, 0.0).astype(jnp.bfloat16)
            total = total + jnp.dot(pick, all_ref[at : at + step, :], preferred_element_type=jnp.float32)
        out[...] = jnp.where(live, total, 0.0).astype(jnp.bfloat16)


def mirror_sum(first, live, mirror, everyone, count):
    total_pairs, width = everyone.shape
    half = count // 2
    smem = pl.BlockSpec(memory_space=pltpu.SMEM)
    vmem = pl.BlockSpec(memory_space=pltpu.VMEM)
    return pl.pallas_call(
        functools.partial(mirror_kernel, step=512),
        in_specs=[smem, smem, vmem, vmem],
        out_specs=[vmem, vmem],
        out_shape=[jax.ShapeDtypeStruct((half, width), jnp.bfloat16)] * 2,
        compiler_params=pltpu.CompilerParams(vmem_limit_bytes=24 << 20),
    )(first, live, mirror.reshape(1, total_pairs), everyone)


def ladder_kernel(tags_ref, place_a, place_b, live_ref, *refs, n_a, n_b, group):
    pieces_a, pieces_b = refs[:n_a], refs[n_a : n_a + n_b]
    w_ref, o_ref, amps_a, amps_b, total, sems = refs[n_a + n_b :]
    share = w_ref.shape[2] // 2
    width = w_ref.shape[3]
    half = total.shape[1] // 2
    step = pl.program_id(0)

    def copies():
        made = []
        for pieces, amps in ((pieces_a, amps_a), (pieces_b, amps_b)):
            at = 0
            for piece in pieces:
                rows = piece.shape[0]
                made.append(
                    pltpu.make_async_copy(piece, amps.at[pl.ds(at, rows), :], sems.at[len(made)])
                )
                at += rows
        return made

    @pl.when(step == 0)
    def _():
        made = copies()
        for copy in made:
            copy.start()
        total[...] = jnp.zeros_like(total)
        for copy in made:
            copy.wait()

    for i in range(group):
        for j in range(2):
            slot = (step * group + i) * 2 + j
            tag = tags_ref[slot]

            @pl.when(tag > 0)
            def _(i=i, j=j, slot=slot, tag=tag):
                weight = w_ref[:, i, j * share : (j + 1) * share, :].reshape(-1, width)
                row = tag - 1
                at_a = pl.multiple_of(place_a[slot] * half, half)
                at_b = pl.multiple_of(place_b[slot] * half, half)
                for at, amps, base in ((at_a, amps_a, 0), (at_b, amps_b, half)):
                    term = lax.dot_general(
                        amps[pl.ds(at, half), :],
                        weight,
                        (((1,), (1,)), ((), ())),
                        preferred_element_type=jnp.float32,
                    )
                    total[row, base : base + half, :] += term

    @pl.when(step == pl.num_programs(0) - 1)
    def _():
        position = lax.broadcasted_iota(jnp.int32, (1, width), 1)
        for r in range(2):
            kept = jnp.where(position < live_ref[r], total[r], 0.0)
            o_ref[:, r * width : (r + 1) * width] = kept.astype(jnp.bfloat16)


def ladder(tags, place_a, place_b, live, pieces_a, pieces_b, weights, count):
    shares, senders, height, width = weights.shape
    group = 4
    n_a, n_b = len(pieces_a), len(pieces_b)
    rows_a = sum(p.shape[0] for p in pieces_a)
    rows_b = sum(p.shape[0] for p in pieces_b)
    return pl.pallas_call(
        functools.partial(ladder_kernel, n_a=n_a, n_b=n_b, group=group),
        grid_spec=pltpu.PrefetchScalarGridSpec(
            num_scalar_prefetch=4,
            grid=(senders // group,),
            in_specs=[pl.BlockSpec(memory_space=pl.ANY)] * (n_a + n_b)
            + [pl.BlockSpec((shares, group, height, width), lambda i, *_: (0, i, 0, 0))],
            out_specs=pl.BlockSpec((count, 2 * width), lambda i, *_: (0, 0)),
            scratch_shapes=[
                pltpu.VMEM((rows_a, width), jnp.bfloat16),
                pltpu.VMEM((rows_b, width), jnp.bfloat16),
                pltpu.VMEM((2, count, width), jnp.float32),
                pltpu.SemaphoreType.DMA((n_a + n_b,)),
            ],
        ),
        out_shape=jax.ShapeDtypeStruct((count, 2 * width), jnp.bfloat16),
        compiler_params=pltpu.CompilerParams(vmem_limit_bytes=32 << 20),
    )(tags, place_a, place_b, live, *pieces_a, *pieces_b, weights)


def local(amplitudes, size_cd, integrals, block_rows, block_cols, size_ab, mirror):
    count, _, width = amplitudes.shape
    owners = lax.axis_size("tile")
    shares = lax.axis_size("pair")
    pair_id = lax.axis_index("pair").astype(jnp.int32)
    tile_id = lax.axis_index("tile").astype(jnp.int32)
    share = width // shares

    everyone = lax.all_gather(amplitudes.reshape(count, width), "pair", axis=0, tiled=True)

    send = route(block_rows, block_cols, pair_id.reshape(1), integrals, owners, shares)
    got = lax.all_to_all(send, "tile", split_axis=0, concat_axis=0, tiled=True)
    weights = lax.all_gather(got[:, : 2 * share, :], "pair", axis=0)
    labels = got[:, 2 * share : 2 * share + 4, 0].astype(jnp.int32)
    tags = labels[:, 0::2].reshape(-1)
    cols = labels[:, 1::2].reshape(-1)
    behind_z = (tile_id // NY - cols // NY) % NZ
    behind_y = (tile_id % NY - cols % NY) % NY

    half_a, half_b = mirror_sum((pair_id * count).reshape(1), size_cd, mirror, everyone, count)
    bundle_a = jnp.concatenate(ring_gather("y", half_a), axis=0)
    bundle_b = jnp.concatenate(ring_gather("z", half_b), axis=0)
    pieces_a = ring_gather("z", bundle_a)
    pieces_b = ring_gather("y", bundle_b)
    result = ladder(
        tags,
        behind_z * NY + behind_y,
        behind_y * NZ + behind_z,
        size_ab,
        pieces_a,
        pieces_b,
        weights,
        count,
    )
    return result.reshape(count, 2, width)


def solution(mesh):
    in_specs = (
        P("pair", "tile", None),
        P("tile"),
        P("tile", None, None),
        P("tile"),
        P("tile"),
        P("tile"),
        P(),
    )
    out_specs = P("pair", "tile", None)
    return jax.shard_map(local, mesh=mesh, in_specs=in_specs, out_specs=out_specs, check_vma=False)
```

```python
import functools

import jax
import jax.numpy as jnp
from jax import lax
from jax.experimental import pallas as pl
from jax.experimental.pallas import tpu as pltpu
from jax.sharding import PartitionSpec as P

NX, NY, NZ = 4, 4, 8
ROWS_A = 256
LABEL_ROWS = 8


def ring_steps(axis, shift):
    if axis == "x":
        return [(2 * x + c, 2 * ((x + shift) % NX) + c) for x in range(NX) for c in range(2)]
    steps = []
    for z in range(NZ):
        for y in range(NY):
            to = ((z + shift) % NZ, y) if axis == "z" else (z, (y + shift) % NY)
            steps.append((z * NY + y, to[0] * NY + to[1]))
    return steps


def ring_gather(axis, piece):
    size = {"x": NX, "y": NY, "z": NZ}[axis]
    name = "pair" if axis == "x" else "tile"
    ahead, back = ring_steps(axis, 1), ring_steps(axis, -1)
    parts = {0: [piece]}
    left = right = piece
    for step in range(1, size // 2):
        left = lax.ppermute(left, name, ahead)
        right = lax.ppermute(right, name, back)
        parts[step], parts[size - step] = [left], [right]
    half = piece.shape[0] // 2
    parts[size // 2] = [
        lax.ppermute(left[:half], name, ahead),
        lax.ppermute(right[half:], name, back),
    ]
    return [parts[s] for s in range(size)]


def flat(parts):
    return [p for part in parts for p in part]


def other_core(piece):
    return lax.ppermute(piece, "pair", [(p, p ^ 1) for p in range(2 * NX)])


def route_kernel(rows_ref, cols_ref, share_ref, w_ref, o_ref, count):
    owners, height, width = o_ref.shape
    blocks, share, _ = w_ref.shape
    o_ref[...] = jnp.zeros_like(o_ref)
    for d in range(owners):
        count[d] = 0
    line = lax.broadcasted_iota(jnp.int32, (LABEL_ROWS, width), 0)
    for b in range(blocks):
        row = rows_ref[b]
        owner = row // 2
        rank = count[owner]
        count[owner] = rank + 1
        o_ref[owner, pl.ds(pl.multiple_of(rank * share, share), share), :] = w_ref[b]
        tags = o_ref[owner, 2 * share :, :].astype(jnp.float32)
        tags = jnp.where(line == 2 * rank, (row % 2 + 1).astype(jnp.float32), tags)
        tags = jnp.where(line == 2 * rank + 1, cols_ref[b].astype(jnp.float32), tags)
        o_ref[owner, 2 * share :, :] = tags.astype(jnp.bfloat16)


def route(block_rows, block_cols, share_id, integrals, owners, shares):
    blocks, height, width = integrals.shape
    share = height // shares
    return pl.pallas_call(
        route_kernel,
        grid_spec=pltpu.PrefetchScalarGridSpec(
            num_scalar_prefetch=3,
            grid=(1,),
            in_specs=[pl.BlockSpec((blocks, share, width), lambda i, r, c, s: (0, s[0], 0))],
            out_specs=pl.BlockSpec((owners, 2 * share + LABEL_ROWS, width), lambda i, r, c, s: (0, 0, 0)),
            scratch_shapes=[pltpu.SMEM((owners,), jnp.int32)],
        ),
        out_shape=jax.ShapeDtypeStruct((owners, 2 * share + LABEL_ROWS, width), jnp.bfloat16),
        compiler_params=pltpu.CompilerParams(vmem_limit_bytes=60 << 20),
    )(block_rows, block_cols, share_id, integrals)


def mirror_kernel(pair_ref, live_ref, mirror_ref, mine_ref, other_ref, a_ref, b_ref):
    rows, width = mine_ref.shape
    count = rows // NX
    live = lax.broadcasted_iota(jnp.int32, (1, width), 1) < live_ref[0]
    me = pair_ref[0]
    start = 0
    for out in (a_ref, b_ref):
        tall = out.shape[0]
        own = lax.broadcasted_iota(jnp.int32, (tall, count), 0) + (me * count + start)
        total = jnp.zeros((tall, width), jnp.float32)
        for core, ref in enumerate((mine_ref, other_ref)):
            for behind in range(NX):
                x = lax.rem(me // 2 + NX - behind, NX)
                source = 2 * x + lax.rem(me + core, 2)
                first = pl.multiple_of(source * count, count)
                here = lax.broadcasted_iota(jnp.int32, (tall, count), 1) + first
                pick = (mirror_ref[:, pl.ds(first, count)] == own) | (here == own)
                pick = jnp.where(pick, 1.0, 0.0).astype(jnp.bfloat16)
                total = total + jnp.dot(
                    pick,
                    ref[behind * count : (behind + 1) * count, :],
                    preferred_element_type=jnp.float32,
                )
        out[...] = jnp.where(live, total, 0.0).astype(jnp.bfloat16)
        start += tall


def mirror_sum(pair_id, live, mirror, mine, other, count):
    width = mine.shape[1]
    smem = pl.BlockSpec(memory_space=pltpu.SMEM)
    vmem = pl.BlockSpec(memory_space=pltpu.VMEM)
    return pl.pallas_call(
        mirror_kernel,
        in_specs=[smem, smem, vmem, vmem, vmem],
        out_specs=[vmem, vmem],
        out_shape=[
            jax.ShapeDtypeStruct((rows, width), jnp.bfloat16) for rows in (ROWS_A, count - ROWS_A)
        ],
        compiler_params=pltpu.CompilerParams(vmem_limit_bytes=24 << 20),
    )(pair_id, live, mirror.reshape(1, -1), mine, other)


def ladder_kernel(tags_ref, place_a, place_b, live_ref, pair_ref, *refs, n_a, n_b, n_w):
    pieces_a, pieces_b = refs[:n_a], refs[n_a : n_a + n_b]
    pieces_w = refs[n_a + n_b : n_a + n_b + n_w]
    o_ref, amps_a, amps_b, weights, total, sems = refs[n_a + n_b + n_w :]
    width = weights.shape[3]
    share = width // weights.shape[0]
    rows_a = amps_a.shape[0] // (NY * NZ)
    rows_b = amps_b.shape[0] // (NY * NZ)
    me = pair_ref[0]
    made = []

    def copy(source, target):
        made.append(pltpu.make_async_copy(source, target, sems.at[len(made)]))
        made[-1].start()

    for pieces, amps in ((pieces_a, amps_a), (pieces_b, amps_b)):
        at = 0
        for piece in pieces:
            copy(piece, amps.at[pl.ds(at, piece.shape[0]), :])
            at += piece.shape[0]
    at = 0
    for piece in pieces_w:
        behind, core = at // weights.shape[1] % NX, at // weights.shape[1] // NX
        source = 2 * lax.rem(me // 2 + NX - behind, NX) + lax.rem(me + core, 2)
        copy(piece, weights.at[source, pl.ds(at % weights.shape[1], piece.shape[0])])
        at += piece.shape[0]
    total[...] = jnp.zeros_like(total)
    for one in made:
        one.wait()

    @pl.loop(0, tags_ref.shape[0] // 2)
    def _(sender):
        for j in range(2):
            slot = sender * 2 + j
            tag = tags_ref[slot]

            @pl.when(tag > 0)
            def _(j=j, slot=slot, tag=tag):
                weight = weights[:, sender, j * share : (j + 1) * share, :].reshape(-1, width)
                row = tag - 1
                base = 0
                for place, amps, rows in ((place_a, amps_a, rows_a), (place_b, amps_b, rows_b)):
                    at = pl.multiple_of(place[slot] * rows, 16)
                    total[row, base : base + rows, :] += lax.dot_general(
                        amps[pl.ds(at, rows), :],
                        weight,
                        (((1,), (1,)), ((), ())),
                        preferred_element_type=jnp.float32,
                    )
                    base += rows

    position = lax.broadcasted_iota(jnp.int32, (1, width), 1)
    for r in range(2):
        kept = jnp.where(position < live_ref[r], total[r], 0.0)
        o_ref[:, r * width : (r + 1) * width] = kept.astype(jnp.bfloat16)


def ladder(tags, place_a, place_b, live, pair_id, pieces_a, pieces_b, pieces_w, count):
    senders, height, width = pieces_w[0].shape
    n_a, n_b, n_w = len(pieces_a), len(pieces_b), len(pieces_w)
    rows_a = sum(p.shape[0] for p in pieces_a)
    rows_b = sum(p.shape[0] for p in pieces_b)
    return pl.pallas_call(
        functools.partial(ladder_kernel, n_a=n_a, n_b=n_b, n_w=n_w),
        in_specs=[pl.BlockSpec(memory_space=pltpu.SMEM)] * 5
        + [pl.BlockSpec(memory_space=pl.ANY)] * (n_a + n_b + n_w),
        out_specs=pl.BlockSpec(memory_space=pltpu.VMEM),
        scratch_shapes=[
            pltpu.VMEM((rows_a, width), jnp.bfloat16),
            pltpu.VMEM((rows_b, width), jnp.bfloat16),
            pltpu.VMEM((2 * NX, senders, height, width), jnp.bfloat16),
            pltpu.VMEM((2, count, width), jnp.float32),
            pltpu.SemaphoreType.DMA((n_a + n_b + n_w,)),
        ],
        out_shape=jax.ShapeDtypeStruct((count, 2 * width), jnp.bfloat16),
        compiler_params=pltpu.CompilerParams(vmem_limit_bytes=60 << 20),
    )(tags, place_a, place_b, live, pair_id, *pieces_a, *pieces_b, *pieces_w)


def local(amplitudes, size_cd, integrals, block_rows, block_cols, size_ab, mirror):
    count, _, width = amplitudes.shape
    owners = lax.axis_size("tile")
    shares = lax.axis_size("pair")
    pair_id = lax.axis_index("pair").astype(jnp.int32)
    tile_id = lax.axis_index("tile").astype(jnp.int32)
    share = width // shares

    send = route(block_rows, block_cols, pair_id.reshape(1), integrals, owners, shares)
    got = lax.all_to_all(send, "tile", split_axis=0, concat_axis=0, tiled=True)

    mine = jnp.concatenate(flat(ring_gather("x", amplitudes.reshape(count, width))), axis=0)
    half_a, half_b = mirror_sum(pair_id.reshape(1), size_cd, mirror, mine, other_core(mine), count)
    bundle_a = jnp.concatenate(flat(ring_gather("y", half_a)), axis=0)
    bundle_b = jnp.concatenate(flat(ring_gather("z", half_b)), axis=0)
    pieces_a = flat(ring_gather("z", bundle_a))
    pieces_b = flat(ring_gather("y", bundle_b))

    shares_x = flat(ring_gather("x", got))
    pieces_w = shares_x + [other_core(p) for p in shares_x]
    labels = got[:, 2 * share : 2 * share + 4, 0].astype(jnp.int32)
    tags = labels[:, 0::2].reshape(-1)
    cols = labels[:, 1::2].reshape(-1)
    behind_z = (tile_id // NY - cols // NY) % NZ
    behind_y = (tile_id % NY - cols % NY) % NY
    result = ladder(
        tags,
        behind_z * NY + behind_y,
        behind_y * NZ + behind_z,
        size_ab,
        pair_id.reshape(1),
        pieces_a,
        pieces_b,
        pieces_w,
        count,
    )
    return result.reshape(count, 2, width)


def solution(mesh):
    in_specs = (
        P("pair", "tile", None),
        P("tile"),
        P("tile", None, None),
        P("tile"),
        P("tile"),
        P("tile"),
        P(),
    )
    out_specs = P("pair", "tile", None)
    return jax.shard_map(local, mesh=mesh, in_specs=in_specs, out_specs=out_specs, check_vma=False)
```

```python
import functools

import jax
import jax.numpy as jnp
from jax import lax
from jax.experimental import pallas as pl
from jax.experimental.pallas import tpu as pltpu
from jax.sharding import PartitionSpec as P

NX, NY, NZ = 4, 4, 8
ROWS_A = 256
LABEL_ROWS = 8


def ring_steps(axis, shift):
    if axis == "x":
        return [(2 * x + c, 2 * ((x + shift) % NX) + c) for x in range(NX) for c in range(2)]
    steps = []
    for z in range(NZ):
        for y in range(NY):
            to = ((z + shift) % NZ, y) if axis == "z" else (z, (y + shift) % NY)
            steps.append((z * NY + y, to[0] * NY + to[1]))
    return steps


def send(axis, shift, piece):
    return lax.ppermute(piece, "pair" if axis == "x" else "tile", ring_steps(axis, shift))


def after(piece, *others):
    return lax.optimization_barrier((piece, *others))[0]


def other_core(piece):
    return lax.ppermute(piece, "pair", [(p, p ^ 1) for p in range(2 * NX)])


def route_kernel(rows_ref, cols_ref, share_ref, w_ref, o_ref, count):
    owners, height, width = o_ref.shape
    blocks, share, _ = w_ref.shape
    o_ref[...] = jnp.zeros_like(o_ref)
    for d in range(owners):
        count[d] = 0
    line = lax.broadcasted_iota(jnp.int32, (LABEL_ROWS, width), 0)
    for b in range(blocks):
        row = rows_ref[b]
        owner = row // 2
        rank = count[owner]
        count[owner] = rank + 1
        o_ref[owner, pl.ds(pl.multiple_of(rank * share, share), share), :] = w_ref[b]
        tags = o_ref[owner, 2 * share :, :].astype(jnp.float32)
        tags = jnp.where(line == 2 * rank, (row % 2 + 1).astype(jnp.float32), tags)
        tags = jnp.where(line == 2 * rank + 1, cols_ref[b].astype(jnp.float32), tags)
        o_ref[owner, 2 * share :, :] = tags.astype(jnp.bfloat16)


def route(block_rows, block_cols, share_id, integrals, owners, shares):
    blocks, height, width = integrals.shape
    share = height // shares
    return pl.pallas_call(
        route_kernel,
        grid_spec=pltpu.PrefetchScalarGridSpec(
            num_scalar_prefetch=3,
            grid=(1,),
            in_specs=[pl.BlockSpec((blocks, share, width), lambda i, r, c, s: (0, s[0], 0))],
            out_specs=pl.BlockSpec((owners, 2 * share + LABEL_ROWS, width), lambda i, r, c, s: (0, 0, 0)),
            scratch_shapes=[pltpu.SMEM((owners,), jnp.int32)],
        ),
        out_shape=jax.ShapeDtypeStruct((owners, 2 * share + LABEL_ROWS, width), jnp.bfloat16),
        compiler_params=pltpu.CompilerParams(vmem_limit_bytes=60 << 20),
    )(block_rows, block_cols, share_id, integrals)


def mirror_kernel(pair_ref, live_ref, mirror_ref, *refs):
    pieces, a_ref, b_ref = refs[:-2], refs[-2], refs[-1]
    count, width = pieces[0].shape
    live = lax.broadcasted_iota(jnp.int32, (1, width), 1) < live_ref[0]
    me = pair_ref[0]
    start = 0
    for out in (a_ref, b_ref):
        tall = out.shape[0]
        own = lax.broadcasted_iota(jnp.int32, (tall, 1), 0) + (me * count + start)
        total = jnp.zeros((tall, width), jnp.float32)
        at = 0
        for ref in pieces:
            height = ref.shape[0]
            behind, core, skip = at // count % NX, at // count // NX, at % count
            source = 2 * lax.rem(me // 2 + NX - behind, NX) + lax.rem(me + core, 2)
            first = pl.multiple_of(source * count + skip, height)
            here = lax.broadcasted_iota(jnp.int32, (tall, height), 1) + first
            pick = (mirror_ref[:, pl.ds(first, height)] == own) | (here == own)
            pick = jnp.where(pick, 1.0, 0.0).astype(jnp.bfloat16)
            total = total + jnp.dot(pick, ref[...], preferred_element_type=jnp.float32)
            at += height
        out[...] = jnp.where(live, total, 0.0).astype(jnp.bfloat16)
        start += tall


def mirror_sum(pair_id, live, mirror, pieces):
    count, width = pieces[0].shape
    smem = pl.BlockSpec(memory_space=pltpu.SMEM)
    vmem = pl.BlockSpec(memory_space=pltpu.VMEM)
    return pl.pallas_call(
        mirror_kernel,
        in_specs=[smem, smem] + [vmem] * (1 + len(pieces)),
        out_specs=[vmem, vmem],
        out_shape=[
            jax.ShapeDtypeStruct((rows, width), jnp.bfloat16) for rows in (ROWS_A, count - ROWS_A)
        ],
        compiler_params=pltpu.CompilerParams(vmem_limit_bytes=24 << 20),
    )(pair_id, live, mirror.reshape(1, -1), *pieces)


def ladder_kernel(tags_ref, place_ref, live_ref, pair_ref, *refs, n_amps):
    pieces, pieces_w = refs[:n_amps], refs[n_amps:-5]
    o_ref, amps, weights, total, sems = refs[-5:]
    senders, width = weights.shape[1], weights.shape[3]
    share = width // weights.shape[0]
    rows = amps.shape[0] // (NY * NZ)
    me = pair_ref[0]
    made = []

    def copy(source, target):
        made.append(pltpu.make_async_copy(source, target, sems.at[len(made)]))
        made[-1].start()

    at = 0
    for piece in pieces:
        copy(piece, amps.at[pl.ds(at, piece.shape[0]), :])
        at += piece.shape[0]
    at = 0
    for piece in pieces_w:
        behind, core = at // senders % NX, at // senders // NX
        source = 2 * lax.rem(me // 2 + NX - behind, NX) + lax.rem(me + core, 2)
        copy(piece, weights.at[source, pl.ds(at % senders, piece.shape[0])])
        at += piece.shape[0]
    total[...] = jnp.zeros_like(total)
    for one in made:
        one.wait()

    @pl.loop(0, senders)
    def _(sender):
        for j in range(2):
            slot = sender * 2 + j
            tag = tags_ref[slot]

            @pl.when(tag > 0)
            def _(j=j, slot=slot, tag=tag):
                weight = weights[:, sender, j * share : (j + 1) * share, :].reshape(-1, width)
                at = pl.multiple_of(place_ref[slot] * rows, 16)
                total[tag - 1] += lax.dot_general(
                    amps[pl.ds(at, rows), :],
                    weight,
                    (((1,), (1,)), ((), ())),
                    preferred_element_type=jnp.float32,
                )

    position = lax.broadcasted_iota(jnp.int32, (1, width), 1)
    for r in range(2):
        kept = jnp.where(position < live_ref[r], total[r], 0.0)
        o_ref[:, r * width : (r + 1) * width] = kept.astype(jnp.bfloat16)


def ladder(tags, place, live, pair_id, pieces, pieces_w):
    senders, height, width = pieces_w[0].shape
    n_amps, n_w = len(pieces), len(pieces_w)
    all_rows = sum(p.shape[0] for p in pieces)
    rows = all_rows // (NY * NZ)
    return pl.pallas_call(
        functools.partial(ladder_kernel, n_amps=n_amps),
        in_specs=[pl.BlockSpec(memory_space=pltpu.SMEM)] * 4
        + [pl.BlockSpec(memory_space=pl.ANY)] * (n_amps + n_w),
        out_specs=pl.BlockSpec(memory_space=pltpu.VMEM),
        scratch_shapes=[
            pltpu.VMEM((all_rows, width), jnp.bfloat16),
            pltpu.VMEM((2 * NX, senders, height, width), jnp.bfloat16),
            pltpu.VMEM((2, rows, width), jnp.float32),
            pltpu.SemaphoreType.DMA((n_amps + n_w,)),
        ],
        out_shape=jax.ShapeDtypeStruct((rows, 2 * width), jnp.bfloat16),
        compiler_params=pltpu.CompilerParams(vmem_limit_bytes=60 << 20),
    )(tags, place, live, pair_id, *pieces, *pieces_w)


def local(amplitudes, size_cd, integrals, block_rows, block_cols, size_ab, mirror):
    count, _, width = amplitudes.shape
    owners = lax.axis_size("tile")
    shares = lax.axis_size("pair")
    pair_id = lax.axis_index("pair").astype(jnp.int32)
    tile_id = lax.axis_index("tile").astype(jnp.int32)
    share = width // shares

    raw = amplitudes.reshape(count, width)
    half = count // 2
    pieces = [
        raw,
        send("x", 1, raw),
        send("x", 2, raw[:half]),
        send("x", -2, raw[half:]),
        send("x", -1, raw),
    ]

    routed = route(block_rows, block_cols, pair_id.reshape(1), integrals, owners, shares)
    got = lax.all_to_all(routed, "tile", split_axis=0, concat_axis=0, tiled=True)

    pieces += [other_core(p) for p in pieces]
    a, b = mirror_sum(pair_id.reshape(1), size_cd, mirror, pieces)

    half = a.shape[0] // 2
    b1, b7 = send("z", 1, b), send("z", -1, b)
    ay = [a, send("y", 1, a), send("y", 2, a[:half]), send("y", -2, a[half:]), send("y", -1, a)]
    a0 = jnp.concatenate(ay, axis=0)
    b2, b6 = send("z", 1, b1), send("z", -1, b7)
    a0 = after(a0, b1, b7)
    a1, a7 = send("z", 1, a0), send("z", -1, a0)
    b3, b5 = send("z", 1, b2), send("z", -1, b6)
    half = b.shape[0] // 2
    b4 = [send("z", 1, b3[:half]), send("z", -1, b5[half:])]
    a1, a7 = after(a1, b3, b5), after(a7, b3, b5)
    a2, a6 = send("z", 1, a1), send("z", -1, a7)
    b0 = jnp.concatenate([b, b1, b2, b3, *b4, b5, b6, b7], axis=0)
    by1, by3 = send("y", 1, b0), send("y", -1, b0)
    a2, a6 = after(a2, *b4), after(a6, *b4)
    a3, a5 = send("z", 1, a2), send("z", -1, a6)
    half = a0.shape[0] // 2
    a4 = [send("z", 1, a3[:half]), send("z", -1, a5[half:])]
    half = b0.shape[0] // 2
    by2 = [send("y", 1, by1[:half]), send("y", -1, by3[half:])]
    pieces_a = [a0, a1, a2, a3, *a4, a5, a6, a7]
    pieces_b = [b0, by1, *by2, by3]

    w1, w3 = send("x", 1, got), send("x", -1, got)
    half = got.shape[0] // 2
    w2 = [send("x", 1, w1[:half]), send("x", -1, w3[half:])]
    pieces_w = [got, w1, *w2, w3]
    pieces_w += [other_core(p) for p in pieces_w]
    labels = got[:, 2 * share : 2 * share + 4, 0].astype(jnp.int32)
    tags = labels[:, 0::2].reshape(-1)
    cols = labels[:, 1::2].reshape(-1)
    behind_z = (tile_id // NY - cols // NY) % NZ
    behind_y = (tile_id % NY - cols % NY) % NY
    above = ladder(tags, behind_z * NY + behind_y, size_ab, pair_id.reshape(1), pieces_a, pieces_w)
    below = ladder(tags, behind_y * NZ + behind_z, size_ab, pair_id.reshape(1), pieces_b, pieces_w)
    return jnp.concatenate([above, below], axis=0).reshape(count, 2, width)


def solution(mesh):
    in_specs = (
        P("pair", "tile", None),
        P("tile"),
        P("tile", None, None),
        P("tile"),
        P("tile"),
        P("tile"),
        P(),
    )
    out_specs = P("pair", "tile", None)
    return jax.shard_map(local, mesh=mesh, in_specs=in_specs, out_specs=out_specs, check_vma=False)
```

```python
import functools

import jax
import jax.numpy as jnp
from jax import lax
from jax.experimental import pallas as pl
from jax.experimental.pallas import tpu as pltpu
from jax.sharding import PartitionSpec as P

NX, NY, NZ = 4, 4, 8
ROWS_A = 208
LABEL_ROWS = 8
GROUP = 4


def ring_steps(axis, shift):
    if axis == "x":
        return [(2 * x + c, 2 * ((x + shift) % NX) + c) for x in range(NX) for c in range(2)]
    steps = []
    for z in range(NZ):
        for y in range(NY):
            to = ((z + shift) % NZ, y) if axis == "z" else (z, (y + shift) % NY)
            steps.append((z * NY + y, to[0] * NY + to[1]))
    return steps


def send(axis, shift, piece):
    return lax.ppermute(piece, "pair" if axis == "x" else "tile", ring_steps(axis, shift))


def after(piece, *others):
    return lax.optimization_barrier((piece, *others))[0]


def other_core(piece):
    return lax.ppermute(piece, "pair", [(p, p ^ 1) for p in range(2 * NX)])


def route_kernel(rows_ref, cols_ref, share_ref, w_ref, o_ref, count):
    owners, height, width = o_ref.shape
    blocks, share, _ = w_ref.shape
    o_ref[...] = jnp.zeros_like(o_ref)
    for d in range(owners):
        count[d] = 0
    line = lax.broadcasted_iota(jnp.int32, (LABEL_ROWS, width), 0)
    for b in range(blocks):
        row = rows_ref[b]
        owner = row // 2
        rank = count[owner]
        count[owner] = rank + 1
        o_ref[owner, pl.ds(pl.multiple_of(rank * share, share), share), :] = w_ref[b]
        tags = o_ref[owner, 2 * share :, :].astype(jnp.float32)
        tags = jnp.where(line == 2 * rank, (row % 2 + 1).astype(jnp.float32), tags)
        tags = jnp.where(line == 2 * rank + 1, cols_ref[b].astype(jnp.float32), tags)
        o_ref[owner, 2 * share :, :] = tags.astype(jnp.bfloat16)


def route(block_rows, block_cols, share_id, integrals, owners, shares):
    blocks, height, width = integrals.shape
    share = height // shares
    return pl.pallas_call(
        route_kernel,
        grid_spec=pltpu.PrefetchScalarGridSpec(
            num_scalar_prefetch=3,
            grid=(1,),
            in_specs=[pl.BlockSpec((blocks, share, width), lambda i, r, c, s: (0, s[0], 0))],
            out_specs=pl.BlockSpec((owners, 2 * share + LABEL_ROWS, width), lambda i, r, c, s: (0, 0, 0)),
            scratch_shapes=[pltpu.SMEM((owners,), jnp.int32)],
        ),
        out_shape=jax.ShapeDtypeStruct((owners, 2 * share + LABEL_ROWS, width), jnp.bfloat16),
        compiler_params=pltpu.CompilerParams(vmem_limit_bytes=60 << 20),
    )(block_rows, block_cols, share_id, integrals)


def mirror_kernel(pair_ref, live_ref, mirror_ref, *refs):
    pieces, a_ref, b_ref = refs[:-2], refs[-2], refs[-1]
    count, width = pieces[0].shape
    live = lax.broadcasted_iota(jnp.int32, (1, width), 1) < live_ref[0]
    me = pair_ref[0]
    start = 0
    for out in (a_ref, b_ref):
        tall = out.shape[0]
        own = lax.broadcasted_iota(jnp.int32, (tall, 1), 0) + (me * count + start)
        total = jnp.zeros((tall, width), jnp.float32)
        at = 0
        for ref in pieces:
            height = ref.shape[0]
            behind, core, skip = at // count % NX, at // count // NX, at % count
            source = 2 * lax.rem(me // 2 + NX - behind, NX) + lax.rem(me + core, 2)
            first = pl.multiple_of(source * count + skip, height)
            here = lax.broadcasted_iota(jnp.int32, (tall, height), 1) + first
            pick = (mirror_ref[:, pl.ds(first, height)] == own) | (here == own)
            pick = jnp.where(pick, 1.0, 0.0).astype(jnp.bfloat16)
            total = total + jnp.dot(pick, ref[...], preferred_element_type=jnp.float32)
            at += height
        out[...] = jnp.where(live, total, 0.0).astype(jnp.bfloat16)
        start += tall


def mirror_sum(pair_id, live, mirror, pieces):
    count, width = pieces[0].shape
    smem = pl.BlockSpec(memory_space=pltpu.SMEM)
    vmem = pl.BlockSpec(memory_space=pltpu.VMEM)
    return pl.pallas_call(
        mirror_kernel,
        in_specs=[smem, smem] + [vmem] * (1 + len(pieces)),
        out_specs=[vmem, vmem],
        out_shape=[
            jax.ShapeDtypeStruct((rows, width), jnp.bfloat16) for rows in (ROWS_A, count - ROWS_A)
        ],
        compiler_params=pltpu.CompilerParams(vmem_limit_bytes=24 << 20),
    )(pair_id, live, mirror.reshape(1, -1), *pieces)


def label_kernel(tile_ref, got_ref, o_ref):
    senders, lanes = o_ref.shape
    start = got_ref.shape[1] - LABEL_ROWS
    labels = got_ref[:, start:, :lanes].astype(jnp.float32)
    lane = lax.broadcasted_iota(jnp.int32, (senders, lanes), 1)
    first = lane % 2 == 0
    tag = jnp.where(first, labels[:, 0], labels[:, 2]).astype(jnp.int32)
    col = jnp.where(first, labels[:, 1], labels[:, 3]).astype(jnp.int32)
    me = tile_ref[0]
    behind_z = (me // NY - col // NY + NZ) % NZ
    behind_y = (me % NY - col % NY + NY) % NY
    o_ref[...] = jnp.where(lane < 2, tag, jnp.where(lane < 4, behind_z, behind_y))


def read_labels(tile_id, got):
    return pl.pallas_call(
        label_kernel,
        in_specs=[pl.BlockSpec(memory_space=pltpu.SMEM), pl.BlockSpec(memory_space=pltpu.VMEM)],
        out_specs=pl.BlockSpec(memory_space=pltpu.VMEM),
        out_shape=jax.ShapeDtypeStruct((got.shape[0], 128), jnp.int32),
        compiler_params=pltpu.CompilerParams(vmem_limit_bytes=8 << 20),
    )(tile_id, got)


def ladder_kernel(label_ref, live_ref, pair_ref, *refs, n_a, n_b):
    pieces_a, pieces_b, pieces_w = refs[:n_a], refs[n_a : n_a + n_b], refs[n_a + n_b : -8]
    o_ref, amps, weights, total, slots, z_list, y_list, sems = refs[-8:]
    senders, width = weights.shape[1] - 1, weights.shape[3]
    share = width // weights.shape[0]
    rows_a = pieces_a[0].shape[1]
    me = pair_ref[0]
    made = []

    def copy(source, target):
        made.append(pltpu.make_async_copy(source, target, sems.at[len(made)]))
        made[-1].start()

    at = 0
    for piece in pieces_w:
        behind, core = at // senders % NX, at // senders // NX
        source = 2 * lax.rem(me // 2 + NX - behind, NX) + lax.rem(me + core, 2)
        copy(piece, weights.at[source, pl.ds(at % senders, piece.shape[0])])
        at += piece.shape[0]
    at = 0
    for piece in pieces_a:
        copy(piece, amps.at[at // NY, pl.ds(at % NY, piece.shape[0]), pl.ds(0, rows_a), :])
        at += piece.shape[0]
    at = 0
    for piece in pieces_b:
        height = piece.shape[1]
        copy(piece, amps.at[pl.ds(at % NZ, piece.shape[0]), at // NZ, pl.ds(rows_a, height), :])
        at += piece.shape[0]

    total[...] = jnp.zeros_like(total)
    weights[:, senders] = jnp.zeros(weights.shape[:1] + weights.shape[2:], weights.dtype)
    room = slots.shape[0] // 2

    def sort(slot, counts):
        tag = label_ref[slot // 2, slot % 2]
        at = jnp.where(tag == 2, room + counts[1], counts[0])

        @pl.when(tag > 0)
        def _():
            slots[at] = slot
            z_list[at] = label_ref[slot // 2, 2 + slot % 2]
            y_list[at] = label_ref[slot // 2, 4 + slot % 2]

        return (
            counts[0] + (tag == 1).astype(jnp.int32),
            counts[1] + (tag == 2).astype(jnp.int32),
        )

    counts = lax.fori_loop(0, 2 * senders, sort, (jnp.int32(0), jnp.int32(0)))
    for r in range(2):
        for i in range(GROUP):
            at = r * room + counts[r] + i
            slots[at] = 2 * senders
            z_list[at] = 0
            y_list[at] = 0

    for one in made:
        one.wait()

    for r in range(2):

        @pl.loop(0, (counts[r] + GROUP - 1) // GROUP)
        def _(g, r=r):
            added = None
            for i in range(GROUP):
                at = r * room + g * GROUP + i
                slot = slots[at]
                low = pl.multiple_of(slot % 2 * share, share)
                weight = weights[:, slot // 2, pl.ds(low, share), :].reshape(-1, width)
                term = lax.dot_general(
                    amps[z_list[at], y_list[at]],
                    weight,
                    (((1,), (1,)), ((), ())),
                    preferred_element_type=jnp.float32,
                )
                added = term if added is None else added + term
            total[r] += added

    position = lax.broadcasted_iota(jnp.int32, (1, width), 1)
    for r in range(2):
        kept = jnp.where(position < live_ref[r], total[r], 0.0)
        o_ref[:, r * width : (r + 1) * width] = kept.astype(jnp.bfloat16)


def ladder(labels, live, pair_id, pieces_a, pieces_b, pieces_w):
    senders, height, width = pieces_w[0].shape
    count = pieces_a[0].shape[1] + pieces_b[0].shape[1]
    n_a, n_b, n_w = len(pieces_a), len(pieces_b), len(pieces_w)
    room = 2 * senders + GROUP
    return pl.pallas_call(
        functools.partial(ladder_kernel, n_a=n_a, n_b=n_b),
        in_specs=[pl.BlockSpec(memory_space=pltpu.SMEM)] * 3
        + [pl.BlockSpec(memory_space=pl.ANY)] * (n_a + n_b + n_w),
        out_specs=pl.BlockSpec(memory_space=pltpu.VMEM),
        scratch_shapes=[
            pltpu.VMEM((NZ, NY, count, width), jnp.bfloat16),
            pltpu.VMEM((2 * NX, senders + 1, height, width), jnp.bfloat16),
            pltpu.VMEM((2, count, width), jnp.float32),
            pltpu.SMEM((2 * room,), jnp.int32),
            pltpu.SMEM((2 * room,), jnp.int32),
            pltpu.SMEM((2 * room,), jnp.int32),
            pltpu.SemaphoreType.DMA((n_a + n_b + n_w,)),
        ],
        out_shape=jax.ShapeDtypeStruct((count, 2 * width), jnp.bfloat16),
        compiler_params=pltpu.CompilerParams(vmem_limit_bytes=60 << 20),
    )(labels, live, pair_id, *pieces_a, *pieces_b, *pieces_w)


def local(amplitudes, size_cd, integrals, block_rows, block_cols, size_ab, mirror):
    count, _, width = amplitudes.shape
    owners = lax.axis_size("tile")
    shares = lax.axis_size("pair")
    pair_id = lax.axis_index("pair").astype(jnp.int32)
    tile_id = lax.axis_index("tile").astype(jnp.int32)
    raw = amplitudes.reshape(count, width)
    half = count // 2
    pieces = [
        raw,
        send("x", 1, raw),
        send("x", 2, raw[:half]),
        send("x", -2, raw[half:]),
        send("x", -1, raw),
    ]

    routed = route(block_rows, block_cols, pair_id.reshape(1), integrals, owners, shares)
    got = lax.all_to_all(after(routed, *pieces[1:]), "tile", split_axis=0, concat_axis=0, tiled=True)

    pieces += [other_core(p) for p in pieces]
    a, b = mirror_sum(pair_id.reshape(1), size_cd, mirror, pieces)

    half = a.shape[0] // 2
    b1, b7 = send("z", 1, b), send("z", -1, b)
    ay = [a, send("y", 1, a), send("y", 2, a[:half]), send("y", -2, a[half:]), send("y", -1, a)]
    a0 = jnp.concatenate(ay, axis=0)
    b2, b6 = send("z", 1, b1), send("z", -1, b7)
    a0 = after(a0, b1, b7)
    a1, a7 = send("z", 1, a0), send("z", -1, a0)
    b3, b5 = send("z", 1, b2), send("z", -1, b6)
    b3, b5 = after(b3, got), after(b5, got)
    half = b.shape[0] // 2
    b4 = [send("z", 1, b3[:half]), send("z", -1, b5[half:])]
    a1, a7 = after(a1, b3, b5), after(a7, b3, b5)
    a2, a6 = send("z", 1, a1), send("z", -1, a7)
    b0 = jnp.concatenate([b, b1, b2, b3, *b4, b5, b6, b7], axis=0)
    by1, by3 = send("y", 1, b0), send("y", -1, b0)
    a2, a6 = after(a2, b0), after(a6, b0)
    a3, a5 = send("z", 1, a2), send("z", -1, a6)
    half = a0.shape[0] // 2
    a4 = [send("z", 1, a3[:half]), send("z", -1, a5[half:])]
    half = b0.shape[0] // 2
    by2 = [send("y", 1, by1[:half]), send("y", -1, by3[half:])]
    pieces_a = [a0, a1, a2, a3, *a4, a5, a6, a7]
    pieces_b = [b0, by1, *by2, by3]

    w1, w3 = send("x", 1, got), send("x", -1, got)
    half = got.shape[0] // 2
    w1, w3 = after(w1, a2, a6), after(w3, a2, a6)
    w2 = [send("x", 1, w1[:half]), send("x", -1, w3[half:])]
    pieces_w = [got, w1, *w2, w3]
    held = [after(p, a3, a5) for p in (got, w1)] + [after(p, *a4) for p in w2] + [after(w3, a3, a5)]
    pieces_w += [other_core(p) for p in held]
    result = ladder(
        read_labels(tile_id.reshape(1), got),
        size_ab,
        pair_id.reshape(1),
        [p.reshape(-1, *a.shape) for p in pieces_a],
        [p.reshape(-1, *b.shape) for p in pieces_b],
        pieces_w,
    )
    return result.reshape(count, 2, width)


def solution(mesh):
    in_specs = (
        P("pair", "tile", None),
        P("tile"),
        P("tile", None, None),
        P("tile"),
        P("tile"),
        P("tile"),
        P(),
    )
    out_specs = P("pair", "tile", None)
    return jax.shard_map(local, mesh=mesh, in_specs=in_specs, out_specs=out_specs, check_vma=False)
```

```python
import functools

import jax
import jax.numpy as jnp
from jax import lax
from jax.experimental import pallas as pl
from jax.experimental.pallas import tpu as pltpu
from jax.sharding import PartitionSpec as P

NX, NY, NZ = 4, 4, 8
ROWS_A = 192
LABEL_ROWS = 8
GROUP = 4
B_RUNS = (
    (0, 0, 0, 3, 0),
    (0, 3, 6, 2, 0),
    (1, 0, 0, 3, 1),
    (1, 3, 6, 2, 1),
    (2, 0, 0, 3, 2),
    (3, 0, 6, 2, 2),
    (4, 0, 0, 3, 3),
    (4, 3, 6, 2, 3),
    (5, 0, 3, 3, 0),
    (6, 0, 3, 3, 1),
    (7, 0, 3, 1, 2),
    (8, 0, 4, 2, 2),
    (9, 0, 3, 3, 3),
)


def ring_steps(axis, shift):
    if axis == "x":
        return [(2 * x + c, 2 * ((x + shift) % NX) + c) for x in range(NX) for c in range(2)]
    steps = []
    for z in range(NZ):
        for y in range(NY):
            to = ((z + shift) % NZ, y) if axis == "z" else (z, (y + shift) % NY)
            steps.append((z * NY + y, to[0] * NY + to[1]))
    return steps


def send(axis, shift, piece):
    return lax.ppermute(piece, "pair" if axis == "x" else "tile", ring_steps(axis, shift))


def after(piece, *others):
    return lax.optimization_barrier((piece, *others))[0]


def other_core(piece):
    return lax.ppermute(piece, "pair", [(p, p ^ 1) for p in range(2 * NX)])


def route_kernel(rows_ref, cols_ref, share_ref, w_ref, o_ref, count):
    owners, height, width = o_ref.shape
    blocks, share, _ = w_ref.shape
    o_ref[...] = jnp.zeros_like(o_ref)
    for d in range(owners):
        count[d] = 0
    line = lax.broadcasted_iota(jnp.int32, (LABEL_ROWS, width), 0)
    for b in range(blocks):
        row = rows_ref[b]
        owner = row // 2
        rank = count[owner]
        count[owner] = rank + 1
        o_ref[owner, pl.ds(pl.multiple_of(rank * share, share), share), :] = w_ref[b]
        tags = o_ref[owner, 2 * share :, :].astype(jnp.float32)
        tags = jnp.where(line == 2 * rank, (row % 2 + 1).astype(jnp.float32), tags)
        tags = jnp.where(line == 2 * rank + 1, cols_ref[b].astype(jnp.float32), tags)
        o_ref[owner, 2 * share :, :] = tags.astype(jnp.bfloat16)


def route(block_rows, block_cols, share_id, integrals, owners, shares):
    blocks, height, width = integrals.shape
    share = height // shares
    return pl.pallas_call(
        route_kernel,
        grid_spec=pltpu.PrefetchScalarGridSpec(
            num_scalar_prefetch=3,
            grid=(1,),
            in_specs=[pl.BlockSpec((blocks, share, width), lambda i, r, c, s: (0, s[0], 0))],
            out_specs=pl.BlockSpec((owners, 2 * share + LABEL_ROWS, width), lambda i, r, c, s: (0, 0, 0)),
            scratch_shapes=[pltpu.SMEM((owners,), jnp.int32)],
        ),
        out_shape=jax.ShapeDtypeStruct((owners, 2 * share + LABEL_ROWS, width), jnp.bfloat16),
        compiler_params=pltpu.CompilerParams(vmem_limit_bytes=60 << 20),
    )(block_rows, block_cols, share_id, integrals)


def mirror_kernel(pair_ref, live_ref, mirror_ref, *refs):
    pieces, a_ref, b_ref = refs[:-2], refs[-2], refs[-1]
    count, width = pieces[0].shape
    live = lax.broadcasted_iota(jnp.int32, (1, width), 1) < live_ref[0]
    me = pair_ref[0]
    start = 0
    for out in (a_ref, b_ref):
        tall = out.shape[0]
        own = lax.broadcasted_iota(jnp.int32, (tall, 1), 0) + (me * count + start)
        total = jnp.zeros((tall, width), jnp.float32)
        at = 0
        for ref in pieces:
            height = ref.shape[0]
            behind, core, skip = at // count % NX, at // count // NX, at % count
            source = 2 * lax.rem(me // 2 + NX - behind, NX) + lax.rem(me + core, 2)
            first = pl.multiple_of(source * count + skip, height)
            here = lax.broadcasted_iota(jnp.int32, (tall, height), 1) + first
            pick = (mirror_ref[:, pl.ds(first, height)] == own) | (here == own)
            pick = jnp.where(pick, 1.0, 0.0).astype(jnp.bfloat16)
            total = total + jnp.dot(pick, ref[...], preferred_element_type=jnp.float32)
            at += height
        out[...] = jnp.where(live, total, 0.0).astype(jnp.bfloat16)
        start += tall


def mirror_sum(pair_id, live, mirror, pieces):
    count, width = pieces[0].shape
    smem = pl.BlockSpec(memory_space=pltpu.SMEM)
    vmem = pl.BlockSpec(memory_space=pltpu.VMEM)
    return pl.pallas_call(
        mirror_kernel,
        in_specs=[smem, smem] + [vmem] * (1 + len(pieces)),
        out_specs=[vmem, vmem],
        out_shape=[
            jax.ShapeDtypeStruct((rows, width), jnp.bfloat16) for rows in (ROWS_A, count - ROWS_A)
        ],
        compiler_params=pltpu.CompilerParams(vmem_limit_bytes=24 << 20),
    )(pair_id, live, mirror.reshape(1, -1), *pieces)


def label_kernel(tile_ref, got_ref, o_ref):
    senders, lanes = o_ref.shape
    start = got_ref.shape[1] - LABEL_ROWS
    labels = got_ref[:, start:, :lanes].astype(jnp.float32)
    lane = lax.broadcasted_iota(jnp.int32, (senders, lanes), 1)
    first = lane % 2 == 0
    tag = jnp.where(first, labels[:, 0], labels[:, 2]).astype(jnp.int32)
    col = jnp.where(first, labels[:, 1], labels[:, 3]).astype(jnp.int32)
    me = tile_ref[0]
    behind_z = (me // NY - col // NY + NZ) % NZ
    behind_y = (me % NY - col % NY + NY) % NY
    o_ref[...] = jnp.where(lane < 2, tag, jnp.where(lane < 4, behind_z, behind_y))


def read_labels(tile_id, got):
    return pl.pallas_call(
        label_kernel,
        in_specs=[pl.BlockSpec(memory_space=pltpu.SMEM), pl.BlockSpec(memory_space=pltpu.VMEM)],
        out_specs=pl.BlockSpec(memory_space=pltpu.VMEM),
        out_shape=jax.ShapeDtypeStruct((got.shape[0], 128), jnp.int32),
        compiler_params=pltpu.CompilerParams(vmem_limit_bytes=8 << 20),
    )(tile_id, got)


def ladder_kernel(label_ref, live_ref, pair_ref, *refs, n_a, n_b):
    pieces_a, pieces_b, pieces_w = refs[:n_a], refs[n_a : n_a + n_b], refs[n_a + n_b : -8]
    o_ref, amps, weights, total, slots, z_list, y_list, sems = refs[-8:]
    senders, width = weights.shape[1] - 1, weights.shape[3]
    share = width // weights.shape[0]
    rows_a = pieces_a[0].shape[1]
    me = pair_ref[0]
    made = []

    def copy(source, target):
        made.append(pltpu.make_async_copy(source, target, sems.at[len(made)]))
        made[-1].start()

    at = 0
    for piece in pieces_w:
        behind, core = at // senders % NX, at // senders // NX
        source = 2 * lax.rem(me // 2 + NX - behind, NX) + lax.rem(me + core, 2)
        copy(piece, weights.at[source, pl.ds(at % senders, piece.shape[0])])
        at += piece.shape[0]
    at = 0
    for piece in pieces_a:
        copy(piece, amps.at[at // NY, pl.ds(at % NY, piece.shape[0]), pl.ds(0, rows_a), :])
        at += piece.shape[0]
    for piece, skip, z, tall, y in B_RUNS:
        height = pieces_b[piece].shape[1]
        copy(
            pieces_b[piece].at[pl.ds(skip, tall)],
            amps.at[pl.ds(z, tall), y, pl.ds(rows_a, height), :],
        )

    total[...] = jnp.zeros_like(total)
    weights[:, senders] = jnp.zeros(weights.shape[:1] + weights.shape[2:], weights.dtype)
    room = slots.shape[0] // 2

    def sort(slot, counts):
        tag = label_ref[slot // 2, slot % 2]
        at = jnp.where(tag == 2, room + counts[1], counts[0])

        @pl.when(tag > 0)
        def _():
            slots[at] = slot
            z_list[at] = label_ref[slot // 2, 2 + slot % 2]
            y_list[at] = label_ref[slot // 2, 4 + slot % 2]

        return (
            counts[0] + (tag == 1).astype(jnp.int32),
            counts[1] + (tag == 2).astype(jnp.int32),
        )

    counts = lax.fori_loop(0, 2 * senders, sort, (jnp.int32(0), jnp.int32(0)))
    for r in range(2):
        for i in range(GROUP):
            at = r * room + counts[r] + i
            slots[at] = 2 * senders
            z_list[at] = 0
            y_list[at] = 0

    for one in made:
        one.wait()

    for r in range(2):

        @pl.loop(0, (counts[r] + GROUP - 1) // GROUP)
        def _(g, r=r):
            added = None
            for i in range(GROUP):
                at = r * room + g * GROUP + i
                slot = slots[at]
                low = pl.multiple_of(slot % 2 * share, share)
                weight = weights[:, slot // 2, pl.ds(low, share), :].reshape(-1, width)
                term = lax.dot_general(
                    amps[z_list[at], y_list[at]],
                    weight,
                    (((1,), (1,)), ((), ())),
                    preferred_element_type=jnp.float32,
                )
                added = term if added is None else added + term
            total[r] += added

    position = lax.broadcasted_iota(jnp.int32, (1, width), 1)
    for r in range(2):
        kept = jnp.where(position < live_ref[r], total[r], 0.0)
        o_ref[:, r * width : (r + 1) * width] = kept.astype(jnp.bfloat16)


def ladder(labels, live, pair_id, pieces_a, pieces_b, pieces_w):
    senders, height, width = pieces_w[0].shape
    count = pieces_a[0].shape[1] + pieces_b[0].shape[1]
    n_a, n_b, n_w = len(pieces_a), len(pieces_b), len(pieces_w)
    room = 2 * senders + GROUP
    return pl.pallas_call(
        functools.partial(ladder_kernel, n_a=n_a, n_b=n_b),
        in_specs=[pl.BlockSpec(memory_space=pltpu.SMEM)] * 3
        + [pl.BlockSpec(memory_space=pl.ANY)] * (n_a + n_b + n_w),
        out_specs=pl.BlockSpec(memory_space=pltpu.VMEM),
        scratch_shapes=[
            pltpu.VMEM((NZ, NY, count, width), jnp.bfloat16),
            pltpu.VMEM((2 * NX, senders + 1, height, width), jnp.bfloat16),
            pltpu.VMEM((2, count, width), jnp.float32),
            pltpu.SMEM((2 * room,), jnp.int32),
            pltpu.SMEM((2 * room,), jnp.int32),
            pltpu.SMEM((2 * room,), jnp.int32),
            pltpu.SemaphoreType.DMA((n_a + len(B_RUNS) + n_w,)),
        ],
        out_shape=jax.ShapeDtypeStruct((count, 2 * width), jnp.bfloat16),
        compiler_params=pltpu.CompilerParams(vmem_limit_bytes=60 << 20),
    )(labels, live, pair_id, *pieces_a, *pieces_b, *pieces_w)


def local(amplitudes, size_cd, integrals, block_rows, block_cols, size_ab, mirror):
    count, _, width = amplitudes.shape
    owners = lax.axis_size("tile")
    shares = lax.axis_size("pair")
    pair_id = lax.axis_index("pair").astype(jnp.int32)
    tile_id = lax.axis_index("tile").astype(jnp.int32)
    raw = amplitudes.reshape(count, width)
    half = count // 2
    pieces = [
        raw,
        send("x", 1, raw),
        send("x", 2, raw[:half]),
        send("x", -2, raw[half:]),
        send("x", -1, raw),
    ]

    routed = route(block_rows, block_cols, pair_id.reshape(1), integrals, owners, shares)

    pieces += [other_core(p) for p in pieces]
    a, b = mirror_sum(pair_id.reshape(1), size_cd, mirror, pieces)
    got = lax.all_to_all(after(routed, *pieces[1:5]), "tile", split_axis=0, concat_axis=0, tiled=True)

    half = a.shape[0] // 2
    b1, b7 = send("z", 1, b), send("z", -1, b)
    ay = [a, send("y", 1, a), send("y", 2, a[:half]), send("y", -2, a[half:]), send("y", -1, a)]
    a0 = jnp.concatenate(ay, axis=0)
    b2, b6 = send("z", 1, b1), send("z", -1, b7)
    a0 = after(a0, b1, b7)
    a1, a7 = send("z", 1, a0), send("z", -1, a0)
    b3, b5 = send("z", 1, b2), send("z", -1, b6)
    near = jnp.concatenate([b, b1, b2, b6, b7], axis=0)
    near1, near3 = send("y", 1, near), send("y", -1, near)
    b3, b5 = after(b3, got), after(b5, got)
    half = b.shape[0] // 2
    b4 = [send("z", 1, b3[:half]), send("z", -1, b5[half:])]
    a1, a7 = after(a1, b3, b5), after(a7, b3, b5)
    a2, a6 = send("z", 1, a1), send("z", -1, a7)
    far = jnp.concatenate([b3, *b4, b5], axis=0)
    far1, far3 = send("y", 1, far), send("y", -1, far)
    a2, a6 = after(a2, far), after(a6, far)
    a3, a5 = send("z", 1, a2), send("z", -1, a6)
    half = a0.shape[0] // 2
    a4 = [send("z", 1, a3[:half]), send("z", -1, a5[half:])]
    rows = b.shape[0]
    near2 = [send("y", 1, near1[: 3 * rows]), send("y", -1, near3[3 * rows :])]
    far2 = [send("y", 1, far1[:rows]), send("y", -1, far3[rows:])]
    pieces_a = [a0, a1, a2, a3, *a4, a5, a6, a7]
    pieces_b = [near, near1, *near2, near3, far, far1, *far2, far3]

    w1, w3 = send("x", 1, got), send("x", -1, got)
    half = got.shape[0] // 2
    w1, w3 = after(w1, a2, a6), after(w3, a2, a6)
    w2 = [send("x", 1, w1[:half]), send("x", -1, w3[half:])]
    pieces_w = [got, w1, *w2, w3]
    held = [after(p, a3, a5) for p in (got, w1)] + [after(p, *a4) for p in w2] + [after(w3, a3, a5)]
    pieces_w += [other_core(p) for p in held]
    result = ladder(
        read_labels(tile_id.reshape(1), got),
        size_ab,
        pair_id.reshape(1),
        [p.reshape(-1, *a.shape) for p in pieces_a],
        [p.reshape(-1, *b.shape) for p in pieces_b],
        pieces_w,
    )
    return result.reshape(count, 2, width)


def solution(mesh):
    in_specs = (
        P("pair", "tile", None),
        P("tile"),
        P("tile", None, None),
        P("tile"),
        P("tile"),
        P("tile"),
        P(),
    )
    out_specs = P("pair", "tile", None)
    return jax.shard_map(local, mesh=mesh, in_specs=in_specs, out_specs=out_specs, check_vma=False)
```

```python
import functools

import jax
import jax.numpy as jnp
from jax import lax
from jax.experimental import pallas as pl
from jax.experimental.pallas import tpu as pltpu
from jax.sharding import PartitionSpec as P

NX, NY, NZ = 4, 4, 8
ROWS_A = 224
LABEL_ROWS = 8
GROUP = 4


def ring_steps(axis, shift):
    if axis == "x":
        return [(2 * x + c, 2 * ((x + shift) % NX) + c) for x in range(NX) for c in range(2)]
    steps = []
    for z in range(NZ):
        for y in range(NY):
            to = ((z + shift) % NZ, y) if axis == "z" else (z, (y + shift) % NY)
            steps.append((z * NY + y, to[0] * NY + to[1]))
    return steps


def send(axis, shift, piece):
    return lax.ppermute(piece, "pair" if axis == "x" else "tile", ring_steps(axis, shift))


def after(piece, *others):
    return lax.optimization_barrier((piece, *others))[0]


def other_core(piece):
    return lax.ppermute(piece, "pair", [(p, p ^ 1) for p in range(2 * NX)])


def route_kernel(rows_ref, cols_ref, share_ref, w_ref, o_ref, count):
    owners, height, width = o_ref.shape
    blocks, share, _ = w_ref.shape
    o_ref[...] = jnp.zeros_like(o_ref)
    for d in range(owners):
        count[d] = 0
    line = lax.broadcasted_iota(jnp.int32, (LABEL_ROWS, width), 0)
    for b in range(blocks):
        row = rows_ref[b]
        owner = row // 2
        rank = count[owner]
        count[owner] = rank + 1
        o_ref[owner, pl.ds(pl.multiple_of(rank * share, share), share), :] = w_ref[b]
        tags = o_ref[owner, 2 * share :, :].astype(jnp.float32)
        tags = jnp.where(line == 2 * rank, (row % 2 + 1).astype(jnp.float32), tags)
        tags = jnp.where(line == 2 * rank + 1, cols_ref[b].astype(jnp.float32), tags)
        o_ref[owner, 2 * share :, :] = tags.astype(jnp.bfloat16)


def route(block_rows, block_cols, share_id, integrals, owners, shares):
    blocks, height, width = integrals.shape
    share = height // shares
    return pl.pallas_call(
        route_kernel,
        grid_spec=pltpu.PrefetchScalarGridSpec(
            num_scalar_prefetch=3,
            grid=(1,),
            in_specs=[pl.BlockSpec((blocks, share, width), lambda i, r, c, s: (0, s[0], 0))],
            out_specs=pl.BlockSpec((owners, 2 * share + LABEL_ROWS, width), lambda i, r, c, s: (0, 0, 0)),
            scratch_shapes=[pltpu.SMEM((owners,), jnp.int32)],
        ),
        out_shape=jax.ShapeDtypeStruct((owners, 2 * share + LABEL_ROWS, width), jnp.bfloat16),
        compiler_params=pltpu.CompilerParams(vmem_limit_bytes=60 << 20),
    )(block_rows, block_cols, share_id, integrals)


def mirror_kernel(pair_ref, live_ref, mirror_ref, *refs):
    pieces, a_ref, b_ref = refs[:-2], refs[-2], refs[-1]
    count, width = pieces[0].shape
    live = lax.broadcasted_iota(jnp.int32, (1, width), 1) < live_ref[0]
    me = pair_ref[0]
    start = 0
    for out in (a_ref, b_ref):
        tall = out.shape[0]
        own = lax.broadcasted_iota(jnp.int32, (tall, 1), 0) + (me * count + start)
        total = jnp.zeros((tall, width), jnp.float32)
        at = 0
        for ref in pieces:
            height = ref.shape[0]
            behind, core, skip = at // count % NX, at // count // NX, at % count
            source = 2 * lax.rem(me // 2 + NX - behind, NX) + lax.rem(me + core, 2)
            first = pl.multiple_of(source * count + skip, height)
            here = lax.broadcasted_iota(jnp.int32, (tall, height), 1) + first
            pick = (mirror_ref[:, pl.ds(first, height)] == own) | (here == own)
            pick = jnp.where(pick, 1.0, 0.0).astype(jnp.bfloat16)
            total = total + jnp.dot(pick, ref[...], preferred_element_type=jnp.float32)
            at += height
        out[...] = jnp.where(live, total, 0.0).astype(jnp.bfloat16)
        start += tall


def mirror_sum(pair_id, live, mirror, pieces):
    count, width = pieces[0].shape
    smem = pl.BlockSpec(memory_space=pltpu.SMEM)
    vmem = pl.BlockSpec(memory_space=pltpu.VMEM)
    return pl.pallas_call(
        mirror_kernel,
        in_specs=[smem, smem] + [vmem] * (1 + len(pieces)),
        out_specs=[vmem, vmem],
        out_shape=[
            jax.ShapeDtypeStruct((rows, width), jnp.bfloat16) for rows in (ROWS_A, count - ROWS_A)
        ],
        compiler_params=pltpu.CompilerParams(vmem_limit_bytes=24 << 20),
    )(pair_id, live, mirror.reshape(1, -1), *pieces)


def label_kernel(tile_ref, got_ref, o_ref):
    senders, lanes = o_ref.shape
    start = got_ref.shape[1] - LABEL_ROWS
    labels = got_ref[:, start:, :lanes].astype(jnp.float32)
    lane = lax.broadcasted_iota(jnp.int32, (senders, lanes), 1)
    first = lane % 2 == 0
    tag = jnp.where(first, labels[:, 0], labels[:, 2]).astype(jnp.int32)
    col = jnp.where(first, labels[:, 1], labels[:, 3]).astype(jnp.int32)
    me = tile_ref[0]
    behind_z = (me // NY - col // NY + NZ) % NZ
    behind_y = (me % NY - col % NY + NY) % NY
    o_ref[...] = jnp.where(lane < 2, tag, jnp.where(lane < 4, behind_z, behind_y))


def read_labels(tile_id, got):
    return pl.pallas_call(
        label_kernel,
        in_specs=[pl.BlockSpec(memory_space=pltpu.SMEM), pl.BlockSpec(memory_space=pltpu.VMEM)],
        out_specs=pl.BlockSpec(memory_space=pltpu.VMEM),
        out_shape=jax.ShapeDtypeStruct((got.shape[0], 128), jnp.int32),
        compiler_params=pltpu.CompilerParams(vmem_limit_bytes=8 << 20),
    )(tile_id, got)


def ladder_kernel(label_ref, live_ref, pair_ref, *refs, n_a, n_b):
    pieces_a, pieces_b, pieces_w = refs[:n_a], refs[n_a : n_a + n_b], refs[n_a + n_b : -8]
    o_ref, amps, weights, total, slots, z_list, y_list, sems = refs[-8:]
    senders, width = weights.shape[1] - 1, weights.shape[3]
    share = width // weights.shape[0]
    rows_a = pieces_a[0].shape[1]
    me = pair_ref[0]
    made = []

    def copy(source, target):
        made.append(pltpu.make_async_copy(source, target, sems.at[len(made)]))
        made[-1].start()

    at = 0
    for piece in pieces_w:
        behind, core = at // senders % NX, at // senders // NX
        source = 2 * lax.rem(me // 2 + NX - behind, NX) + lax.rem(me + core, 2)
        copy(piece, weights.at[source, pl.ds(at % senders, piece.shape[0])])
        at += piece.shape[0]
    at = 0
    for piece in pieces_a:
        copy(piece, amps.at[at // NY, pl.ds(at % NY, piece.shape[0]), pl.ds(0, rows_a), :])
        at += piece.shape[0]
    at = 0
    for piece in pieces_b:
        height = piece.shape[1]
        copy(piece, amps.at[pl.ds(at % NZ, piece.shape[0]), at // NZ, pl.ds(rows_a, height), :])
        at += piece.shape[0]

    total[...] = jnp.zeros_like(total)
    weights[:, senders] = jnp.zeros(weights.shape[:1] + weights.shape[2:], weights.dtype)
    room = slots.shape[0] // 2

    def sort(slot, counts):
        tag = label_ref[slot // 2, slot % 2]
        at = jnp.where(tag == 2, room + counts[1], counts[0])

        @pl.when(tag > 0)
        def _():
            slots[at] = slot
            z_list[at] = label_ref[slot // 2, 2 + slot % 2]
            y_list[at] = label_ref[slot // 2, 4 + slot % 2]

        return (
            counts[0] + (tag == 1).astype(jnp.int32),
            counts[1] + (tag == 2).astype(jnp.int32),
        )

    counts = lax.fori_loop(0, 2 * senders, sort, (jnp.int32(0), jnp.int32(0)))
    for r in range(2):
        for i in range(GROUP):
            at = r * room + counts[r] + i
            slots[at] = 2 * senders
            z_list[at] = 0
            y_list[at] = 0

    for one in made:
        one.wait()

    for r in range(2):

        @pl.loop(0, (counts[r] + GROUP - 1) // GROUP)
        def _(g, r=r):
            added = None
            for i in range(GROUP):
                at = r * room + g * GROUP + i
                slot = slots[at]
                low = pl.multiple_of(slot % 2 * share, share)
                weight = weights[:, slot // 2, pl.ds(low, share), :].reshape(-1, width)
                term = lax.dot_general(
                    amps[z_list[at], y_list[at]],
                    weight,
                    (((1,), (1,)), ((), ())),
                    preferred_element_type=jnp.float32,
                )
                added = term if added is None else added + term
            total[r] += added

    position = lax.broadcasted_iota(jnp.int32, (1, width), 1)
    for r in range(2):
        kept = jnp.where(position < live_ref[r], total[r], 0.0)
        o_ref[:, r * width : (r + 1) * width] = kept.astype(jnp.bfloat16)


def ladder(labels, live, pair_id, pieces_a, pieces_b, pieces_w):
    senders, height, width = pieces_w[0].shape
    count = pieces_a[0].shape[1] + pieces_b[0].shape[1]
    n_a, n_b, n_w = len(pieces_a), len(pieces_b), len(pieces_w)
    room = 2 * senders + GROUP
    return pl.pallas_call(
        functools.partial(ladder_kernel, n_a=n_a, n_b=n_b),
        in_specs=[pl.BlockSpec(memory_space=pltpu.SMEM)] * 3
        + [pl.BlockSpec(memory_space=pl.ANY)] * (n_a + n_b + n_w),
        out_specs=pl.BlockSpec(memory_space=pltpu.VMEM),
        scratch_shapes=[
            pltpu.VMEM((NZ, NY, count, width), jnp.bfloat16),
            pltpu.VMEM((2 * NX, senders + 1, height, width), jnp.bfloat16),
            pltpu.VMEM((2, count, width), jnp.float32),
            pltpu.SMEM((2 * room,), jnp.int32),
            pltpu.SMEM((2 * room,), jnp.int32),
            pltpu.SMEM((2 * room,), jnp.int32),
            pltpu.SemaphoreType.DMA((n_a + n_b + n_w,)),
        ],
        out_shape=jax.ShapeDtypeStruct((count, 2 * width), jnp.bfloat16),
        compiler_params=pltpu.CompilerParams(vmem_limit_bytes=60 << 20),
    )(labels, live, pair_id, *pieces_a, *pieces_b, *pieces_w)


def local(amplitudes, size_cd, integrals, block_rows, block_cols, size_ab, mirror):
    count, _, width = amplitudes.shape
    owners = lax.axis_size("tile")
    shares = lax.axis_size("pair")
    pair_id = lax.axis_index("pair").astype(jnp.int32)
    tile_id = lax.axis_index("tile").astype(jnp.int32)
    raw = amplitudes.reshape(count, width)
    half = count // 2
    pieces = [
        raw,
        send("x", 1, raw),
        send("x", 2, raw[:half]),
        send("x", -2, raw[half:]),
        send("x", -1, raw),
    ]

    routed = route(block_rows, block_cols, pair_id.reshape(1), integrals, owners, shares)
    got = lax.all_to_all(routed, "tile", split_axis=0, concat_axis=0, tiled=True)

    pieces += [other_core(p) for p in pieces]
    a, b = mirror_sum(pair_id.reshape(1), size_cd, mirror, pieces)

    half = a.shape[0] // 2
    b1, b7 = send("z", 1, b), send("z", -1, b)
    ay = [a, send("y", 1, a), send("y", 2, a[:half]), send("y", -2, a[half:]), send("y", -1, a)]
    a0 = jnp.concatenate(ay, axis=0)
    b2, b6 = send("z", 1, b1), send("z", -1, b7)
    a0 = after(a0, b2, b6)
    a1, a7 = send("z", 1, a0), send("z", -1, a0)
    b3, b5 = send("z", 1, b2), send("z", -1, b6)
    b3, b5 = after(b3, got), after(b5, got)
    half = b.shape[0] // 2
    b4 = [send("z", 1, b3[:half]), send("z", -1, b5[half:])]
    a1, a7 = after(a1, *b4), after(a7, *b4)
    a2, a6 = send("z", 1, a1), send("z", -1, a7)
    b0 = jnp.concatenate([b, b1, b2, b3, *b4, b5, b6, b7], axis=0)
    by1, by3 = send("y", 1, b0), send("y", -1, b0)
    a2, a6 = after(a2, b0), after(a6, b0)
    a3, a5 = send("z", 1, a2), send("z", -1, a6)
    half = a0.shape[0] // 2
    a4 = [send("z", 1, a3[:half]), send("z", -1, a5[half:])]
    half = b0.shape[0] // 2
    by2 = [send("y", 1, by1[:half]), send("y", -1, by3[half:])]
    pieces_a = [a0, a1, a2, a3, *a4, a5, a6, a7]
    pieces_b = [b0, by1, *by2, by3]

    w1, w3 = send("x", 1, got), send("x", -1, got)
    half = got.shape[0] // 2
    w1, w3 = after(w1, a2, a6), after(w3, a2, a6)
    w2 = [send("x", 1, w1[:half]), send("x", -1, w3[half:])]
    pieces_w = [got, w1, *w2, w3]
    held = [after(p, a3, a5) for p in (got, w1)] + [after(p, *a4) for p in w2] + [after(w3, a3, a5)]
    pieces_w += [other_core(p) for p in held]
    result = ladder(
        read_labels(tile_id.reshape(1), got),
        size_ab,
        pair_id.reshape(1),
        [p.reshape(-1, *a.shape) for p in pieces_a],
        [p.reshape(-1, *b.shape) for p in pieces_b],
        pieces_w,
    )
    return result.reshape(count, 2, width)


def solution(mesh):
    in_specs = (
        P("pair", "tile", None),
        P("tile"),
        P("tile", None, None),
        P("tile"),
        P("tile"),
        P("tile"),
        P(),
    )
    out_specs = P("pair", "tile", None)
    return jax.shard_map(local, mesh=mesh, in_specs=in_specs, out_specs=out_specs, check_vma=False)
```

```python
import functools

import jax
import jax.numpy as jnp
from jax import lax
from jax.experimental import pallas as pl
from jax.experimental.pallas import tpu as pltpu
from jax.sharding import PartitionSpec as P

NX, NY, NZ = 4, 4, 8
ROWS_A = 240
LABEL_ROWS = 8
GROUP = 4


B_RUNS = (
    *((p, skip, z, tall, y) for p, y in ((0, 0), (1, 1), (4, 3)) for skip, z, tall in ((0, 6, 2), (2, 0, 3), (5, 5, 1), (6, 3, 2))),
    (2, 0, 6, 2, 2),
    (2, 2, 0, 2, 2),
    (3, 0, 2, 1, 2),
    (3, 1, 5, 1, 2),
    (3, 2, 3, 2, 2),
)


def ring_steps(axis, shift):
    if axis == "x":
        return [(2 * x + c, 2 * ((x + shift) % NX) + c) for x in range(NX) for c in range(2)]
    steps = []
    for z in range(NZ):
        for y in range(NY):
            to = ((z + shift) % NZ, y) if axis == "z" else (z, (y + shift) % NY)
            steps.append((z * NY + y, to[0] * NY + to[1]))
    return steps


def send(axis, shift, piece):
    return lax.ppermute(piece, "pair" if axis == "x" else "tile", ring_steps(axis, shift))


def after(piece, *others):
    return lax.optimization_barrier((piece, *others))[0]


def other_core(piece):
    return lax.ppermute(piece, "pair", [(p, p ^ 1) for p in range(2 * NX)])


def route_kernel(rows_ref, cols_ref, share_ref, w_ref, o_ref, count):
    owners, height, width = o_ref.shape
    blocks, share, _ = w_ref.shape
    o_ref[...] = jnp.zeros_like(o_ref)
    for d in range(owners):
        count[d] = 0
    line = lax.broadcasted_iota(jnp.int32, (LABEL_ROWS, width), 0)
    for b in range(blocks):
        row = rows_ref[b]
        owner = row // 2
        rank = count[owner]
        count[owner] = rank + 1
        o_ref[owner, pl.ds(pl.multiple_of(rank * share, share), share), :] = w_ref[b]
        tags = o_ref[owner, 2 * share :, :].astype(jnp.float32)
        tags = jnp.where(line == 2 * rank, (row % 2 + 1).astype(jnp.float32), tags)
        tags = jnp.where(line == 2 * rank + 1, cols_ref[b].astype(jnp.float32), tags)
        o_ref[owner, 2 * share :, :] = tags.astype(jnp.bfloat16)


def route(block_rows, block_cols, share_id, integrals, owners, shares):
    blocks, height, width = integrals.shape
    share = height // shares
    return pl.pallas_call(
        route_kernel,
        grid_spec=pltpu.PrefetchScalarGridSpec(
            num_scalar_prefetch=3,
            grid=(1,),
            in_specs=[pl.BlockSpec((blocks, share, width), lambda i, r, c, s: (0, s[0], 0))],
            out_specs=pl.BlockSpec((owners, 2 * share + LABEL_ROWS, width), lambda i, r, c, s: (0, 0, 0)),
            scratch_shapes=[pltpu.SMEM((owners,), jnp.int32)],
        ),
        out_shape=jax.ShapeDtypeStruct((owners, 2 * share + LABEL_ROWS, width), jnp.bfloat16),
        compiler_params=pltpu.CompilerParams(vmem_limit_bytes=60 << 20),
    )(block_rows, block_cols, share_id, integrals)


def mirror_kernel(pair_ref, live_ref, mirror_ref, *refs):
    pieces, a_ref, b_ref = refs[:-2], refs[-2], refs[-1]
    count, width = pieces[0].shape
    live = lax.broadcasted_iota(jnp.int32, (1, width), 1) < live_ref[0]
    me = pair_ref[0]
    start = 0
    for out in (a_ref, b_ref):
        tall = out.shape[0]
        own = lax.broadcasted_iota(jnp.int32, (tall, 1), 0) + (me * count + start)
        total = jnp.zeros((tall, width), jnp.float32)
        at = 0
        for ref in pieces:
            height = ref.shape[0]
            behind, core, skip = at // count % NX, at // count // NX, at % count
            source = 2 * lax.rem(me // 2 + NX - behind, NX) + lax.rem(me + core, 2)
            first = pl.multiple_of(source * count + skip, height)
            here = lax.broadcasted_iota(jnp.int32, (tall, height), 1) + first
            pick = (mirror_ref[:, pl.ds(first, height)] == own) | (here == own)
            pick = jnp.where(pick, 1.0, 0.0).astype(jnp.bfloat16)
            total = total + jnp.dot(pick, ref[...], preferred_element_type=jnp.float32)
            at += height
        out[...] = jnp.where(live, total, 0.0).astype(jnp.bfloat16)
        start += tall


def mirror_sum(pair_id, live, mirror, pieces):
    count, width = pieces[0].shape
    smem = pl.BlockSpec(memory_space=pltpu.SMEM)
    vmem = pl.BlockSpec(memory_space=pltpu.VMEM)
    return pl.pallas_call(
        mirror_kernel,
        in_specs=[smem, smem] + [vmem] * (1 + len(pieces)),
        out_specs=[vmem, vmem],
        out_shape=[
            jax.ShapeDtypeStruct((rows, width), jnp.bfloat16) for rows in (ROWS_A, count - ROWS_A)
        ],
        compiler_params=pltpu.CompilerParams(vmem_limit_bytes=24 << 20),
    )(pair_id, live, mirror.reshape(1, -1), *pieces)


def label_kernel(tile_ref, got_ref, o_ref):
    senders, lanes = o_ref.shape
    start = got_ref.shape[1] - LABEL_ROWS
    labels = got_ref[:, start:, :lanes].astype(jnp.float32)
    lane = lax.broadcasted_iota(jnp.int32, (senders, lanes), 1)
    first = lane % 2 == 0
    tag = jnp.where(first, labels[:, 0], labels[:, 2]).astype(jnp.int32)
    col = jnp.where(first, labels[:, 1], labels[:, 3]).astype(jnp.int32)
    me = tile_ref[0]
    behind_z = (me // NY - col // NY + NZ) % NZ
    behind_y = (me % NY - col % NY + NY) % NY
    o_ref[...] = jnp.where(lane < 2, tag, jnp.where(lane < 4, behind_z, behind_y))


def read_labels(tile_id, got):
    return pl.pallas_call(
        label_kernel,
        in_specs=[pl.BlockSpec(memory_space=pltpu.SMEM), pl.BlockSpec(memory_space=pltpu.VMEM)],
        out_specs=pl.BlockSpec(memory_space=pltpu.VMEM),
        out_shape=jax.ShapeDtypeStruct((got.shape[0], 128), jnp.int32),
        compiler_params=pltpu.CompilerParams(vmem_limit_bytes=8 << 20),
    )(tile_id, got)


def ladder_kernel(label_ref, live_ref, pair_ref, *refs, n_a, n_b):
    pieces_a, pieces_b, pieces_w = refs[:n_a], refs[n_a : n_a + n_b], refs[n_a + n_b : -8]
    o_ref, amps, weights, total, slots, z_list, y_list, sems = refs[-8:]
    senders, width = weights.shape[1] - 1, weights.shape[3]
    share = width // weights.shape[0]
    rows_a = pieces_a[0].shape[1]
    me = pair_ref[0]
    made = []

    def copy(source, target):
        made.append(pltpu.make_async_copy(source, target, sems.at[len(made)]))
        made[-1].start()

    at = 0
    for piece in pieces_w:
        behind, core = at // senders % NX, at // senders // NX
        source = 2 * lax.rem(me // 2 + NX - behind, NX) + lax.rem(me + core, 2)
        copy(piece, weights.at[source, pl.ds(at % senders, piece.shape[0])])
        at += piece.shape[0]
    at = 0
    for piece in pieces_a:
        copy(piece, amps.at[at // NY, pl.ds(at % NY, piece.shape[0]), pl.ds(0, rows_a), :])
        at += piece.shape[0]
    for piece, skip, z, tall, y in B_RUNS:
        height = pieces_b[piece].shape[1]
        copy(
            pieces_b[piece].at[pl.ds(skip, tall)],
            amps.at[pl.ds(z, tall), y, pl.ds(rows_a, height), :],
        )

    total[...] = jnp.zeros_like(total)
    weights[:, senders] = jnp.zeros(weights.shape[:1] + weights.shape[2:], weights.dtype)
    room = slots.shape[0] // 2

    def sort(slot, counts):
        tag = label_ref[slot // 2, slot % 2]
        at = jnp.where(tag == 2, room + counts[1], counts[0])

        @pl.when(tag > 0)
        def _():
            slots[at] = slot
            z_list[at] = label_ref[slot // 2, 2 + slot % 2]
            y_list[at] = label_ref[slot // 2, 4 + slot % 2]

        return (
            counts[0] + (tag == 1).astype(jnp.int32),
            counts[1] + (tag == 2).astype(jnp.int32),
        )

    counts = lax.fori_loop(0, 2 * senders, sort, (jnp.int32(0), jnp.int32(0)))
    for r in range(2):
        for i in range(GROUP):
            at = r * room + counts[r] + i
            slots[at] = 2 * senders
            z_list[at] = 0
            y_list[at] = 0

    for one in made:
        one.wait()

    for r in range(2):

        @pl.loop(0, (counts[r] + GROUP - 1) // GROUP)
        def _(g, r=r):
            added = None
            for i in range(GROUP):
                at = r * room + g * GROUP + i
                slot = slots[at]
                low = pl.multiple_of(slot % 2 * share, share)
                weight = weights[:, slot // 2, pl.ds(low, share), :].reshape(-1, width)
                term = lax.dot_general(
                    amps[z_list[at], y_list[at]],
                    weight,
                    (((1,), (1,)), ((), ())),
                    preferred_element_type=jnp.float32,
                )
                added = term if added is None else added + term
            total[r] += added

    position = lax.broadcasted_iota(jnp.int32, (1, width), 1)
    for r in range(2):
        kept = jnp.where(position < live_ref[r], total[r], 0.0)
        o_ref[:, r * width : (r + 1) * width] = kept.astype(jnp.bfloat16)


def ladder(labels, live, pair_id, pieces_a, pieces_b, pieces_w):
    senders, height, width = pieces_w[0].shape
    count = pieces_a[0].shape[1] + pieces_b[0].shape[1]
    n_a, n_b, n_w = len(pieces_a), len(pieces_b), len(pieces_w)
    room = 2 * senders + GROUP
    return pl.pallas_call(
        functools.partial(ladder_kernel, n_a=n_a, n_b=n_b),
        in_specs=[pl.BlockSpec(memory_space=pltpu.SMEM)] * 3
        + [pl.BlockSpec(memory_space=pl.ANY)] * (n_a + n_b + n_w),
        out_specs=pl.BlockSpec(memory_space=pltpu.VMEM),
        scratch_shapes=[
            pltpu.VMEM((NZ, NY, count, width), jnp.bfloat16),
            pltpu.VMEM((2 * NX, senders + 1, height, width), jnp.bfloat16),
            pltpu.VMEM((2, count, width), jnp.float32),
            pltpu.SMEM((2 * room,), jnp.int32),
            pltpu.SMEM((2 * room,), jnp.int32),
            pltpu.SMEM((2 * room,), jnp.int32),
            pltpu.SemaphoreType.DMA((n_a + len(B_RUNS) + n_w,)),
        ],
        out_shape=jax.ShapeDtypeStruct((count, 2 * width), jnp.bfloat16),
        compiler_params=pltpu.CompilerParams(vmem_limit_bytes=60 << 20),
    )(labels, live, pair_id, *pieces_a, *pieces_b, *pieces_w)


def local(amplitudes, size_cd, integrals, block_rows, block_cols, size_ab, mirror):
    count, _, width = amplitudes.shape
    owners = lax.axis_size("tile")
    shares = lax.axis_size("pair")
    pair_id = lax.axis_index("pair").astype(jnp.int32)
    tile_id = lax.axis_index("tile").astype(jnp.int32)
    raw = amplitudes.reshape(count, width)
    half = count // 2
    pieces = [
        raw,
        send("x", 1, raw),
        send("x", 2, raw[:half]),
        send("x", -2, raw[half:]),
        send("x", -1, raw),
    ]

    routed = route(block_rows, block_cols, pair_id.reshape(1), integrals, owners, shares)
    got = lax.all_to_all(routed, "tile", split_axis=0, concat_axis=0, tiled=True)

    pieces += [other_core(p) for p in pieces]
    a, b = mirror_sum(pair_id.reshape(1), size_cd, mirror, pieces)

    half = a.shape[0] // 2
    b1, b7 = send("z", 1, b), send("z", -1, b)
    ay = [a, send("y", 1, a), send("y", 2, a[:half]), send("y", -2, a[half:]), send("y", -1, a)]
    a0 = jnp.concatenate(ay, axis=0)
    b2, b6 = send("z", 1, b1), send("z", -1, b7)
    a0 = after(a0, b2, b6)
    a1, a7 = send("z", 1, a0), send("z", -1, a0)
    b3, b5 = send("z", 1, b2), send("z", -1, b6)
    b3, b5 = after(b3, got), after(b5, got)
    half = b.shape[0] // 2
    b4 = [send("z", 1, b3[:half]), send("z", -1, b5[half:])]
    a1, a7 = after(a1, *b4), after(a7, *b4)
    a2, a6 = send("z", 1, a1), send("z", -1, a7)
    b0 = jnp.concatenate([b6, b7, b, b1, b2, b5, b3, *b4], axis=0)
    by1, by3 = send("y", 1, b0), send("y", -1, b0)
    a2, a6 = after(a2, b0), after(a6, b0)
    a3, a5 = send("z", 1, a2), send("z", -1, a6)
    half = a0.shape[0] // 2
    a4 = [send("z", 1, a3[:half]), send("z", -1, a5[half:])]
    half = b0.shape[0] // 2
    by2 = [send("y", 1, by1[:half]), send("y", -1, by3[half:])]
    pieces_a = [a0, a1, a2, a3, *a4, a5, a6, a7]
    pieces_b = [b0, by1, *by2, by3]

    w1, w3 = send("x", 1, got), send("x", -1, got)
    half = got.shape[0] // 2
    w1, w3 = after(w1, a2, a6), after(w3, a2, a6)
    w2 = [send("x", 1, w1[:half]), send("x", -1, w3[half:])]
    pieces_w = [got, w1, *w2, w3]
    held = [after(p, a3, a5) for p in (got, w1)] + [after(p, *a4, *by2) for p in w2] + [after(w3, a3, a5)]
    pieces_w += [other_core(p) for p in held]
    result = ladder(
        read_labels(tile_id.reshape(1), got),
        size_ab,
        pair_id.reshape(1),
        [p.reshape(-1, *a.shape) for p in pieces_a],
        [p.reshape(-1, *b.shape) for p in pieces_b],
        pieces_w,
    )
    return result.reshape(count, 2, width)


def solution(mesh):
    in_specs = (
        P("pair", "tile", None),
        P("tile"),
        P("tile", None, None),
        P("tile"),
        P("tile"),
        P("tile"),
        P(),
    )
    out_specs = P("pair", "tile", None)
    return jax.shard_map(local, mesh=mesh, in_specs=in_specs, out_specs=out_specs, check_vma=False)
```
